32 devices in a mesh: dp: 8 (over z, x), tensor: 4 (over y, core).
Axes of the slice: x: 2, y: 2, z: 4, core: 2. Of those that a mesh axis runs over, the one named last changes fastest.
Arguments:
- inputs: bfloat16 [8192, 768], P(('dp', 'tensor')), may hold values from -6 to 6
- first_gain: bfloat16 [768], P('dp'), may hold values from 0.25 to 1.75
- qkv_weight: bfloat16 [768, 12, 192], P('dp', 'tensor'), may hold values from -0.21875 to 0.21875
- out_weight: bfloat16 [768, 768], P('tensor', 'dp'), may hold values from -0.875 to 0.875
- bias_table: bfloat16 [32, 12], P(None, 'tensor'), may hold values from -4 to 4
- second_gain: bfloat16 [768], P('dp'), may hold values from 0.25 to 1.75
- router_weight: bfloat16 [768, 8], P('dp'), may hold values from -0.15625 to 0.15625
- expert_in: bfloat16 [8, 768, 3072], P('dp', None, 'tensor'), may hold values from -0.21875 to 0.21875
- expert_output_weights: bfloat16 [8, 3072, 768], P('dp', 'tensor'), may hold values from -0.15625 to 0.15625
- segments: int32 [8, 1024], P('dp'), may hold values from 0 to 2, never falling along the last dimension, each value on 1 to 512 neighbouring positions
- buckets: int32 [1024], replicated, may hold values from 0 to 31, as said below
- choices: int32 [8192, 2], P(('dp', 'tensor')), may hold values from 0 to 7, all different within a row; in each aligned block of 256 rows (0 to 255, 256 to 511, ...) at most 128 rows name the same one
- cotangent: bfloat16 [8192, 768], P(('dp', 'tensor')), may hold values from -6 to 6
Outputs:
- result: float32 [8192, 768], P(('dp', 'tensor'))
- grad_inputs: float32 [8192, 768], P(('dp', 'tensor'))
- grad_first_gain: float32 [768], P(('dp', 'tensor'))
- grad_qkv_weight: float32 [768, 12, 192], P('dp', 'tensor')
- grad_out_weight: float32 [768, 768], P('tensor', 'dp')
- grad_bias_table: float32 [32, 12], P(None, 'tensor')
- gradient_second_norm_gain: float32 [768], P(('dp', 'tensor'))
- grad_router_weight: float32 [768, 8], P(('dp', 'tensor'))
- grad_expert_in: float32 [8, 768, 3072], P('dp', None, 'tensor')
- grad_expert_out: float32 [8, 3072, 768], P('dp', 'tensor')
The draws below stay inside these ranges and needn't reach their ends.
Inputs may be any that keep to these rules, and one draw needn't show every extreme that they name: `choices`: within each aligned block of 256 rows (the rows of one device) no expert is named by more than 128 rows; a row names two different experts. `buckets`: never falling with the distance; 0 at distance 0 and 31 at distance 1024 - 1. `segments`: never falling along a sequence; every document has 1 to 512 positions.
All inputs are finite; a program needn't handle non-finite values.
Results may differ from the reference program's by a relative error of at most 0.02.
Values may be sent and summed in bfloat16 or wider, within the bound.
A program may use at most 192 MiB of HBM per device.

```python
import math
from functools import partial
import jax
import jax.numpy as jnp
import numpy as np
from jax import lax

D = 768
HEADS = 12
HEAD_DIM = 64
FF = 3072
TOP = 2
BUCKETS = 32
SEQ_LEN = 1024
TOK_DEV = 256
EXPERTS = 8
TOKENS = 8192
SEQS = 8
CAP = 128
N_TENSOR = 4


def draw_buckets(key, part):
    key = jax.random.fold_in(key, 7)
    random_ids = jax.random.randint(key, (SEQ_LEN,), 0, BUCKETS).astype(jnp.int32)
    random_ids = random_ids.at[0].set(0).at[1].set(BUCKETS - 1)
    return jnp.sort(random_ids).astype(jnp.int32)


def levels(own_key, extent, split, low, high):
    loudness, own = 1.0, jax.random.fold_in(own_key, 6)
    for dim, parts in split:
        steps = jnp.exp(jax.random.uniform(jax.random.fold_in(own, dim), (parts,), jnp.float32, low / len(split), high / len(split)))
        loudness = loudness * jnp.repeat(steps, extent[dim] // parts).reshape([-1 if axis == dim else 1 for axis in range(len(extent))])
    return loudness


def profile(count, total, limit, lean):
    loads = [(1 << 20) // math.isqrt(rank ** lean) + 1 for rank in range(2, count + 1)]
    surplus, holding = total - limit - (count - 1), [1] * (count - 1)
    while surplus > 0:
        candidates = [i for i in range(count - 1) if holding[i] < limit]
        whole, budget = sum([loads[i] for i in candidates]), surplus
        for i in candidates:
            extra = min(limit - holding[i], max(1, budget * loads[i] // whole), surplus)
            holding[i] = holding[i] + extra
            surplus = surplus - extra
    return np.array([limit] + holding)


def ragged_sizes(rng, number_of, total, reach, skew):
    if number_of == 2:
        one = jax.random.randint(rng, (), max(1, total - reach), min(reach, total - 1) + 1)
        return jnp.stack([one, total - one])
    sizes = jnp.asarray(profile(number_of, total, reach, skew), jnp.int32)
    twos = (number_of - 1) // 2
    source_of, taker = sizes[1:1 + 2 * twos:2], sizes[2:2 + 2 * twos:2]
    margin = jnp.minimum(source_of - 1, reach - taker)
    moved = jax.random.randint(jax.random.fold_in(rng, 1), (twos,), 0, 1 << 20) % (margin + 1)
    sizes = sizes.at[1:1 + 2 * twos:2].set(source_of - moved).at[2:2 + 2 * twos:2].set(taker + moved)
    return sizes[jax.random.permutation(jax.random.fold_in(rng, 2), number_of)]


def routed_block(rng, own, number, rows, number_of, top, reach, slope):
    order = jax.random.permutation(rng, number_of)
    heavy_load, ordinary = portions_of(number_of, rows * top, reach, slope, True), portions_of(number_of, rows * top, reach, slope, False)
    places = jnp.arange(number_of)

    def named(tallies, rotation):
        used = int((tallies > 0).sum())
        fixed = max(1, used // 4)
        passed = fixed + (places - fixed + rotation * (used - fixed)) % max(1, number_of - fixed)
        return jnp.zeros((number_of,), jnp.int32).at[order[jnp.where(places < fixed, places, passed)]].set(jnp.asarray(tallies, jnp.int32))

    tallies = jnp.where(number % 4 == 0, named(heavy_load, number // 4), named(ordinary, number - number // 4 - 1))
    mixed = jax.random.permutation(jax.random.fold_in(own, 3), number_of)
    donor, sink = mixed[0:number_of // 2 * 2:2], mixed[1:number_of // 2 * 2:2]
    room = jnp.minimum(tallies[donor] - 1, reach - tallies[sink]) // 2
    room = jnp.where((donor == order[0]) | (sink == order[0]) | (tallies[sink] == 0), 0, jnp.maximum(room, 0))
    passed = jax.random.randint(jax.random.fold_in(own, 4), (number_of // 2,), 0, 1 << 20) % (room + 1)
    tallies = tallies.at[donor].add(-passed).at[sink].add(passed)
    labels = jnp.searchsorted(jnp.cumsum(tallies), jnp.arange(rows * top), side="right").astype(jnp.int32)
    table = labels.reshape(top, rows).T
    table = table[jax.random.permutation(jax.random.fold_in(own, 1), rows)]
    rotation = jax.random.randint(jax.random.fold_in(own, 2), (rows, 1), 0, top)
    return jnp.take_along_axis(table, (jnp.arange(top)[None, :] + rotation) % top, axis=1)


def portions_of(amount, total, bound, slope, full):
    weights = [(1 << 20) // math.isqrt(rank ** slope) + 1 for rank in range(1, amount + 1)]
    largest = bound if full else min(bound, max(-(-total // amount), total * weights[0] // sum(weights)))
    least = 1 if total - largest >= amount - 1 else 0
    given, rest = [largest] + [least] * (amount - 1), total - largest - least * (amount - 1)
    while rest > 0:
        candidates = [i for i in range(1, amount) if given[i] < largest] or [i for i in range(1, amount) if given[i] < bound]
        pool, remaining = sum([weights[i] for i in candidates]), rest
        for i in candidates:
            extra = min(bound - given[i], max(1, remaining * weights[i] // pool), rest)
            given[i] = given[i] + extra
            rest = rest - extra
    return np.array(given)


def noise(stream_key, dims, deviation, reach, split=(), kind=jnp.bfloat16):
    values = jax.random.normal(stream_key, dims, jnp.float32) * deviation
    if len(split) > 0:
        values = levels(stream_key, dims, split, -0.22, 0.18) * values
    return jnp.clip(values, min=-reach, max=reach).astype(kind)


def setup_inputs(seed: int = 0) -> dict:
    arg_keys = jax.random.split(jax.random.key(seed), 14)
    inputs = noise(arg_keys[0], (TOKENS, D), 1.0, 6.0, ((0, 32),))
    first_gain = jnp.clip(1.0 + 0.15 * jax.random.normal(arg_keys[1], (D,), jnp.float32), 0.25, 1.75).astype(jnp.bfloat16)
    qkv_weight = noise(arg_keys[2], (D, HEADS, 3 * HEAD_DIM), D ** -0.5, 0.21875, ((0, 8), (1, 4)))
    out_weight = noise(arg_keys[3], (HEADS * HEAD_DIM, D), (D // 16) ** -0.5, 0.875, ((0, 4), (1, 8)))
    bias_table = noise(arg_keys[4], (BUCKETS, HEADS), 1.0, 4.0, ((1, 4),))
    second_gain = jnp.clip(1.0 + 0.15 * jax.random.normal(arg_keys[5], (D,), jnp.float32), 0.25, 1.75).astype(jnp.bfloat16)
    router_weight = noise(arg_keys[6], (D, EXPERTS), (2 * D) ** -0.5, 0.15625, ((0, 8),))
    expert_in = noise(arg_keys[7], (EXPERTS, D, FF), D ** -0.5, 0.21875, ((0, 8), (2, 4)))
    expert_output_weights = noise(arg_keys[8], (EXPERTS, FF, D), (FF // 2) ** -0.5, 0.15625, ((0, 8), (1, 4)))
    segments = jax.vmap(lambda own: jnp.searchsorted(jnp.cumsum(ragged_sizes(own, 3, SEQ_LEN, SEQ_LEN // 2, 1)), jnp.arange(SEQ_LEN), side="right"))(jax.random.split(arg_keys[9], SEQS)).reshape((SEQS, SEQ_LEN)).astype(jnp.int32)
    buckets = draw_buckets(jax.random.fold_in(arg_keys[13], 71), 0)
    choices_keys = jax.random.split(jax.random.fold_in(arg_keys[11], 1), TOKENS // TOK_DEV)
    choices_turns = jax.random.permutation(jax.random.fold_in(arg_keys[11], 3), TOKENS // TOK_DEV)
    choices = jax.vmap(lambda own, number: routed_block(jax.random.fold_in(arg_keys[11], 2), own, number, TOK_DEV, EXPERTS, TOP, CAP, 1))(choices_keys, choices_turns).reshape((TOKENS, TOP))
    cotangent = noise(arg_keys[12], (TOKENS, D), 1.0, 6.0, ((0, 32),))
    return dict(inputs=inputs, first_gain=first_gain, qkv_weight=qkv_weight, out_weight=out_weight, bias_table=bias_table, second_gain=second_gain, router_weight=router_weight, expert_in=expert_in, expert_output_weights=expert_output_weights, segments=segments, buckets=buckets, choices=choices, cotangent=cotangent)


@jax.custom_vjp
def low(v):
    return lax.optimization_barrier(v.astype(jnp.bfloat16)).astype(jnp.float32)

@jax.custom_vjp
def low_back(v):
    return v

def low_keep(v):
    return (low(v), None)

def low_pass(kept, grad):
    return (grad,)

def back_keep(v):
    return (v, None)

def back_low(kept, grad):
    return (low(grad),)
low.defvjp(low_keep, low_pass)
low_back.defvjp(back_keep, back_low)
EPSILON = 1e-06
MASKED = -1e+30
HIGHEST = lax.Precision.HIGHEST

def rms_norm(values, gain_vec):
    return values * lax.rsqrt(lax.optimization_barrier(jnp.mean(values * values, axis=-1, keepdims=True)) + EPSILON) * gain_vec

def slot_table(expert_ids, num_experts):
    flat_ids = expert_ids.reshape(-1)
    onehot = (flat_ids[:, None] == jnp.arange(num_experts, dtype=jnp.int32)[None, :]).astype(jnp.int32)
    before = jnp.cumsum(onehot, axis=0) - onehot
    return lax.optimization_barrier(jnp.sum(before * onehot, axis=1)).reshape(expert_ids.shape).astype(jnp.int32)

def sequence_attention(packed, qkv_weight, out_weight, bias_full):
    sequence_token_rows, seg_ids = packed
    qkv_all = jnp.einsum('td,dhe->hte', sequence_token_rows, qkv_weight, precision=HIGHEST)
    qkv_all = low(low_back(qkv_all))
    queries = qkv_all[..., :HEAD_DIM]
    key_rows = qkv_all[..., HEAD_DIM:2 * HEAD_DIM]
    value_rows = qkv_all[..., 2 * HEAD_DIM:]
    scores = jnp.einsum('hqe,hke->hqk', queries, key_rows, precision=HIGHEST) * HEAD_DIM ** (-0.5) + bias_full
    scores = low_back(scores)
    position = jnp.arange(SEQ_LEN, dtype=jnp.int32)
    allowed = (position[None, :] <= position[:, None]) & (seg_ids[:, None] == seg_ids[None, :])
    scores = jnp.where(allowed[None], scores, MASKED)
    weights = jax.nn.softmax(scores, axis=-1)
    mixed_out = jnp.einsum('hqk,hke->qhe', low(weights), value_rows, precision=HIGHEST)
    mixed_out = low(low_back(mixed_out)).reshape(SEQ_LEN, HEADS * HEAD_DIM)
    return low_back(jnp.dot(mixed_out, out_weight, precision=HIGHEST))

def expert_apply(packed):
    expert_token_rows, weight_in, weight_out = packed
    quarter = FF // N_TENSOR
    running = jnp.zeros((expert_token_rows.shape[0], D), jnp.float32)
    for quarter_idx in range(N_TENSOR):
        upward = jnp.dot(low_back(expert_token_rows), weight_in[:, quarter_idx * quarter:(quarter_idx + 1) * quarter], precision=HIGHEST)
        active = low(jax.nn.gelu(low_back(upward)))
        running = running + low(jnp.dot(active, weight_out[quarter_idx * quarter:(quarter_idx + 1) * quarter], precision=HIGHEST))
    return running

def reference(inputs, first_gain, qkv_weight, out_weight, bias_table, second_gain, router_weight, expert_in, expert_output_weights, segments, buckets, choices, cotangent):
    position = jnp.arange(SEQ_LEN, dtype=jnp.int32)
    distance = jnp.maximum(position[:, None] - position[None, :], 0)
    bucket_grid = buckets[distance]
    blocks = TOKENS // TOK_DEV
    picked_ids = choices.reshape(blocks, TOK_DEV, TOP)
    slot_ids = jax.vmap(partial(slot_table, num_experts=EXPERTS))(picked_ids)
    block_ids = jnp.arange(blocks, dtype=jnp.int32)[:, None, None]
    target = (picked_ids * (blocks * CAP) + block_ids * CAP + slot_ids).reshape(TOKENS * TOP).astype(jnp.int32)
    pair_ids = (jnp.arange(TOKENS * TOP, dtype=jnp.int32) // TOP).astype(jnp.int32)
    source = jnp.full((EXPERTS * blocks * CAP,), TOKENS, jnp.int32).at[target].set(pair_ids)

    def forward(inputs_f, first_f, qkv_f, out_f, bias_table_float, second_f, router_f, expin_f, expout_f):
        normed_one = low(rms_norm(inputs_f, first_f))
        bias_full = jnp.transpose(bias_table_float[bucket_grid], (2, 0, 1))
        seq_inputs = normed_one.reshape(SEQS, SEQ_LEN, D)

        def attend_one(packed):
            return sequence_attention(packed, qkv_f, out_f, bias_full)
        attended = lax.map(jax.checkpoint(attend_one), (seq_inputs, segments))
        hidden = inputs_f + attended.reshape(TOKENS, D)
        normed_two = low(rms_norm(hidden, second_f))
        logits = low_back(jnp.dot(normed_two, router_f, precision=HIGHEST))
        router_probs = jax.nn.softmax(logits, axis=-1)
        picked = jnp.take_along_axis(router_probs, choices, axis=1)
        gate_values = picked / lax.optimization_barrier(jnp.sum(picked, axis=1, keepdims=True))
        padded = jnp.concatenate([normed_two, jnp.zeros((1, D), jnp.float32)], axis=0)
        rows_all = padded[source].reshape(EXPERTS, blocks * CAP, D)
        expert_rows = lax.map(jax.checkpoint(expert_apply), (rows_all, expin_f, expout_f))
        expert_rows = low_back(expert_rows)
        per_choice = expert_rows.reshape(EXPERTS * blocks * CAP, D)[target].reshape(TOKENS, TOP, D)
        return hidden + lax.optimization_barrier(jnp.sum(gate_values[..., None] * per_choice, axis=1))
    arrays = [inputs, first_gain, qkv_weight, out_weight, bias_table, second_gain, router_weight, expert_in, expert_output_weights]
    arrays = [item.astype(jnp.float32) for item in arrays]
    result, pullback = jax.vjp(forward, *arrays)
    gradients = pullback(cotangent.astype(jnp.float32))
    return (result, gradients[0], gradients[1], gradients[2], gradients[3], gradients[4], gradients[5], gradients[6], gradients[7], gradients[8])
```

```python
import functools

import jax
import jax.numpy as jnp
from jax import lax
from jax.experimental import pallas as pl
from jax.experimental.pallas import tpu as pltpu
from jax.sharding import PartitionSpec as P

EPSILON = 1e-06
MASKED = -1e30
TILE = 256
F32 = jnp.float32
BF16 = jnp.bfloat16


def rms_scale(values):
    return lax.rsqrt(jnp.mean(values * values, axis=-1, keepdims=True) + EPSILON)


def dot_nn(a, b):
    return lax.dot_general(a, b, (((1,), (0,)), ((), ())), preferred_element_type=F32)


def dot_nt(a, b):
    return lax.dot_general(a, b, (((1,), (1,)), ((), ())), preferred_element_type=F32)


def dot_tn(a, b):
    return lax.dot_general(a, b, (((0,), (0,)), ((), ())), preferred_element_type=F32)


def tile_mask(segc_ref, segr_ref, start, keys):
    rows = start + lax.broadcasted_iota(jnp.int32, (TILE, keys), 0)
    cols = lax.broadcasted_iota(jnp.int32, (TILE, keys), 1)
    same = segc_ref[start : start + TILE, :] == segr_ref[:, :keys]
    return (cols <= rows) & same


def toeplitz(rv_row, length):
    return pltpu.roll(
        jnp.broadcast_to(rv_row, (TILE, length)), length - TILE + 1, 1, stride=1, stride_axis=0
    )


def attend_kernel(
    head_dim, x_ref, w_ref, rv_ref, segc_ref, segr_ref, part_ref, qkv_ref, o_ref, lse_ref, acc_ref
):
    head = pl.program_id(0)
    length = x_ref.shape[0]
    w = w_ref[0]
    qkv = dot_nn(x_ref[...], w[:, : 3 * head_dim]).astype(BF16)
    qkv_ref[0] = qkv
    scaled = qkv[:, :head_dim] * jnp.asarray(head_dim ** (-0.5), BF16)
    keys = qkv[:, head_dim : 2 * head_dim]
    vals = qkv[:, 2 * head_dim :]
    bias = toeplitz(rv_ref[0], length)
    for start in range(0, length, TILE):
        stop = start + TILE
        s = dot_nt(scaled[start:stop], keys[:stop]) + bias[:, length - stop :]
        s = jnp.where(tile_mask(segc_ref, segr_ref, start, stop), s, MASKED)
        top = jnp.max(s, axis=-1, keepdims=True)
        e = jnp.exp(s - top)
        total = jnp.sum(e, axis=-1, keepdims=True)
        p = (e * (1.0 / total)).astype(BF16)
        o_ref[0, start:stop, :] = dot_nn(p, vals[:stop]).astype(BF16)
        lse_ref[0, start:stop, :] = top + jnp.log(total)
    out_t = w[:, 3 * head_dim :]
    part = dot_nt(o_ref[0], out_t)

    @pl.when(head == 0)
    def _():
        acc_ref[...] = part

    @pl.when(head > 0)
    def _():
        acc_ref[...] += part

    @pl.when(head == pl.num_programs(0) - 1)
    def _():
        part_ref[...] = acc_ref[...].astype(BF16)


def attend_back_kernel(
    head_dim,
    x_ref,
    g_ref,
    w_ref,
    rv_ref,
    segc_ref,
    segr_ref,
    qkv_ref,
    o_ref,
    lse_ref,
    xin_ref,
    r1_ref,
    dx_ref,
    gw_ref,
    drv_ref,
    gfirst_ref,
    acc_ref,
    diag_ref,
    dqkv_ref,
):
    head = pl.program_id(0)
    length = x_ref.shape[0]
    w = w_ref[0]
    qkv = qkv_ref[0]
    factor = head_dim ** (-0.5)
    grad_o = dot_nn(g_ref[...], w[:, 3 * head_dim :]).astype(BF16)
    scaled = qkv[:, :head_dim] * jnp.asarray(factor, BF16)
    keys = qkv[:, head_dim : 2 * head_dim]
    vals = qkv[:, 2 * head_dim :]
    bias = toeplitz(rv_ref[0], length)
    dkv = [None] * (length // TILE)
    diag_ref[...] = jnp.zeros_like(diag_ref)
    for start in range(0, length, TILE):
        stop = start + TILE
        s = dot_nt(scaled[start:stop], keys[:stop]) + bias[:, length - stop :]
        s = jnp.where(tile_mask(segc_ref, segr_ref, start, stop), s, MASKED)
        p = jnp.exp(s - lse_ref[0, start:stop, :])
        do = grad_o[start:stop]
        dp = dot_nt(do, vals[:stop])
        delta = jnp.sum(p * dp, axis=-1, keepdims=True)
        ds = (p * (dp - delta)).astype(BF16)
        diag_ref[:, length - stop :] += ds.astype(F32)
        dqkv_ref[start:stop, :head_dim] = dot_nn(ds, keys[:stop]) * factor
        dk = dot_tn(ds, scaled[start:stop])
        dv = dot_tn(p.astype(BF16), do)
        both = jnp.concatenate([dk, dv], axis=1)
        if start == 0:
            dqkv_ref[:stop, head_dim:] = both
        else:
            dqkv_ref[:start, head_dim:] += both[:start]
            dqkv_ref[start:stop, head_dim:] = both[start:]
    x = diag_ref[...]
    half = TILE // 2
    while half >= 8:
        x = x[:half] + pltpu.roll(x[half : 2 * half], length - half, 1)
        half //= 2
    total = x[0:1]
    for row in range(1, 8):
        total = total + pltpu.roll(x[row : row + 1], length - row, 1)
    drv_ref[0] = pltpu.roll(total, TILE - 1, 1)
    dqkv = dqkv_ref[...].astype(BF16)
    gw_ref[0, :, : 3 * head_dim] = dot_tn(x_ref[...], dqkv).astype(gw_ref.dtype)
    gw_ref[0, :, 3 * head_dim :] = dot_tn(g_ref[...], o_ref[0]).astype(gw_ref.dtype)
    part = dot_nt(dqkv, w[:, : 3 * head_dim])

    @pl.when(head == 0)
    def _():
        acc_ref[...] = part

    @pl.when(head > 0)
    def _():
        acc_ref[...] += part

    @pl.when(head == pl.num_programs(0) - 1)
    def _():
        full = acc_ref[...]
        dx_ref[...] = full.astype(BF16)
        gfirst_ref[...] = jnp.sum(
            full * (xin_ref[...].astype(F32) * r1_ref[...]), axis=0, keepdims=True
        )


def whole(shape):
    return pl.BlockSpec(shape, lambda h: (0,) * len(shape))


def by_head(shape):
    return pl.BlockSpec((1,) + shape, lambda h: (h,) + (0,) * len(shape))


def attend(x, w, rv, segc, segr, head_dim):
    heads = w.shape[0]
    length, width = x.shape
    return pl.pallas_call(
        functools.partial(attend_kernel, head_dim),
        grid=(heads,),
        in_specs=[
            whole(x.shape),
            by_head(w.shape[1:]),
            by_head((1, length)),
            whole(segc.shape),
            whole(segr.shape),
        ],
        out_specs=[
            whole(x.shape),
            by_head((length, 3 * head_dim)),
            by_head((length, head_dim)),
            by_head((length, 1)),
        ],
        out_shape=[
            jax.ShapeDtypeStruct(x.shape, BF16),
            jax.ShapeDtypeStruct((heads, length, 3 * head_dim), BF16),
            jax.ShapeDtypeStruct((heads, length, head_dim), BF16),
            jax.ShapeDtypeStruct((heads, length, 1), F32),
        ],
        scratch_shapes=[pltpu.VMEM(x.shape, F32)],
        compiler_params=pltpu.CompilerParams(vmem_limit_bytes=40 * 2**20),
        cost_estimate=pl.CostEstimate(
            flops=15_000_000_000, bytes_accessed=8_000_000, transcendentals=2_000_000
        ),
    )(x, w, rv, segc, segr)


def attend_back(x, g, w, rv, segc, segr, qkv, o, lse, xin, r1, head_dim):
    heads = w.shape[0]
    length, width = x.shape
    return pl.pallas_call(
        functools.partial(attend_back_kernel, head_dim),
        grid=(heads,),
        in_specs=[
            whole(x.shape),
            whole(g.shape),
            by_head(w.shape[1:]),
            by_head((1, length)),
            whole(segc.shape),
            whole(segr.shape),
            by_head(qkv.shape[1:]),
            by_head(o.shape[1:]),
            by_head(lse.shape[1:]),
            whole(xin.shape),
            whole(r1.shape),
        ],
        out_specs=[
            whole(x.shape),
            by_head(w.shape[1:]),
            by_head((1, length)),
            whole((1, width)),
        ],
        out_shape=[
            jax.ShapeDtypeStruct(x.shape, BF16),
            jax.ShapeDtypeStruct(w.shape, BF16),
            jax.ShapeDtypeStruct((heads, 1, length), F32),
            jax.ShapeDtypeStruct((1, width), F32),
        ],
        scratch_shapes=[
            pltpu.VMEM(x.shape, F32),
            pltpu.VMEM((TILE, length), F32),
            pltpu.VMEM((length, 3 * head_dim), F32),
        ],
        compiler_params=pltpu.CompilerParams(vmem_limit_bytes=48 * 2**20),
        cost_estimate=pl.CostEstimate(
            flops=30_000_000_000, bytes_accessed=16_000_000, transcendentals=2_000_000
        ),
    )(x, g, w, rv, segc, segr, qkv, o, lse, xin, r1)


def swap_dp(rows):
    return lax.all_to_all(rows, "dp", split_axis=0, concat_axis=0, tiled=True)


def body(
    inputs,
    first_gain,
    qkv_weight,
    out_weight,
    bias_table,
    second_gain,
    router_weight,
    expert_in,
    expert_output_weights,
    segments,
    buckets,
    choices,
    cotangent,
):
    tokens_dev, model_width = inputs.shape
    n_dp = lax.axis_size("dp")
    n_tensor = lax.axis_size("tensor")
    rows_dp, heads_dev, triple = qkv_weight.shape
    head_dim = triple // 3
    experts = router_weight.shape[1]
    seq_len = segments.shape[1]
    bucket_count = bias_table.shape[0]
    top_count = choices.shape[1]
    capacity = max(2, 2 * top_count * tokens_dev // experts)
    slots = experts * capacity

    xin = lax.all_gather(inputs, "tensor", axis=0, tiled=True)
    packed = jnp.concatenate(
        [
            jnp.concatenate(
                [
                    qkv_weight,
                    jnp.transpose(out_weight).reshape(rows_dp, heads_dev, head_dim),
                ],
                axis=2,
            ).reshape(rows_dp, heads_dev * 4 * head_dim),
            first_gain[:, None],
            second_gain[:, None],
            router_weight,
        ],
        axis=1,
    )
    shared = lax.all_gather(packed, "dp", axis=0, tiled=True)
    wide = heads_dev * 4 * head_dim
    w_heads = jnp.transpose(
        shared[:, :wide].reshape(model_width, heads_dev, 4 * head_dim), (1, 0, 2)
    )
    first_f = shared[:, wide].astype(F32)
    second_f = shared[:, wide + 1].astype(F32)
    router_full = shared[:, wide + 2 :]

    ein, eout, xin = lax.optimization_barrier((expert_in, expert_output_weights, xin))
    w_in = lax.all_gather(ein, "tensor", axis=0, tiled=True)
    w_out = lax.all_gather(eout, "tensor", axis=0, tiled=True)

    onehot_bucket = buckets[:, None] == jnp.arange(bucket_count, dtype=jnp.int32)[None, :]
    by_gap = jnp.sum(
        jnp.where(onehot_bucket[:, None, :], jnp.transpose(bias_table)[None].astype(F32), 0.0),
        axis=2,
    )
    rv = jnp.transpose(by_gap[::-1])[:, None, :]

    xin_f = xin.astype(F32)
    r1_all = rms_scale(xin_f)
    xn1 = (xin_f * r1_all * first_f).astype(BF16)
    segc = segments.reshape(seq_len, 1)
    segr = segments.reshape(1, seq_len)
    part, qkv, mixed, lse = attend(xn1, w_heads, rv, segc, segr, head_dim)
    attn = lax.psum_scatter(part, "tensor", scatter_dimension=0, tiled=True).astype(F32)

    input_f = inputs.astype(F32)
    hidden = input_f + attn
    second_scale = rms_scale(hidden)
    normed_two = (hidden * second_scale * second_f).astype(BF16)
    logits = jnp.dot(normed_two, router_full, preferred_element_type=F32)
    probs = jax.nn.softmax(logits, axis=-1)

    pair_count = tokens_dev * top_count
    expert_range = jnp.arange(experts, dtype=jnp.int32)
    named = choices[:, :, None] == expert_range[None, None, :]
    named_flat = named.reshape(pair_count, experts)
    order = jnp.arange(pair_count, dtype=jnp.int32)
    earlier = (order[:, None] > order[None, :]).astype(BF16)
    before = jnp.dot(earlier, named_flat.astype(BF16), preferred_element_type=F32)
    slot = jnp.sum(jnp.where(named_flat, before, 0.0), axis=1).astype(jnp.int32)
    target = choices * capacity + slot.reshape(choices.shape)
    slot_range = jnp.arange(slots, dtype=jnp.int32)
    places = [(target[:, k : k + 1] == slot_range[None, :]).astype(BF16) for k in range(top_count)]

    picked = jnp.sum(jnp.where(named, probs[:, None, :], 0.0), axis=2)
    gate_sum = jnp.sum(picked, axis=1, keepdims=True)
    gates = picked / gate_sum
    grad_out = cotangent.astype(F32)

    send_rows = dot_tn(sum(places[1:], places[0]), normed_two).astype(BF16)
    grad_pairs = jnp.concatenate(
        [(gates[:, k : k + 1] * grad_out).astype(BF16) for k in range(top_count)], axis=0
    )
    send_grad = dot_tn(jnp.concatenate(places, axis=0), grad_pairs).astype(BF16)
    rows = swap_dp(send_rows.reshape(experts, capacity, model_width))
    grads = swap_dp(send_grad.reshape(experts, capacity, model_width))
    rows = rows.reshape(slots, model_width)
    grads = grads.reshape(slots, model_width)

    up = jnp.einsum("rd,qdf->qrf", rows, w_in, preferred_element_type=F32)
    active = jax.nn.gelu(up).astype(BF16)
    y = jnp.einsum("qrf,qfd->rd", active, w_out, preferred_element_type=F32).astype(BF16)
    y_back = swap_dp(y.reshape(experts, capacity, model_width)).reshape(slots, model_width)
    grad_active = jnp.einsum("rd,qfd->qrf", grads, w_out, preferred_element_type=F32)
    grad_up = jax.vjp(jax.nn.gelu, up)[1](grad_active)[0].astype(BF16)
    grad_rows = jnp.einsum("qrf,qdf->rd", grad_up, w_in, preferred_element_type=F32).astype(BF16)
    grad_back = swap_dp(grad_rows.reshape(experts, capacity, model_width))
    grad_back = grad_back.reshape(slots, model_width)
    part_out = jnp.einsum("qrf,rd->qfd", active, grads, preferred_element_type=F32).astype(BF16)
    part_in = jnp.einsum("rd,qrf->qdf", rows, grad_up, preferred_element_type=F32).astype(BF16)

    per_choice = [dot_nn(place, y_back) for place in places]
    result = hidden + sum(gates[:, k : k + 1] * per_choice[k] for k in range(top_count))
    grad_gate = jnp.concatenate(
        [jnp.sum(item * grad_out, axis=1, keepdims=True) for item in per_choice], axis=1
    )
    grad_picked = (grad_gate - jnp.sum(gates * grad_gate, axis=1, keepdims=True)) / gate_sum
    grad_probs = jnp.sum(jnp.where(named, grad_picked[:, :, None], 0.0), axis=1)
    grad_logits = (
        probs * (grad_probs - jnp.sum(probs * grad_probs, axis=1, keepdims=True))
    ).astype(BF16)
    grad_router = dot_tn(normed_two, grad_logits)
    grad_normed = dot_nt(grad_logits, router_full) + dot_nn(
        sum(places[1:], places[0]), grad_back
    )
    weighted = grad_normed * second_f
    scaled_hidden = hidden * second_scale
    grad_second = jnp.sum(grad_normed * scaled_hidden, axis=0)
    grad_hidden = (
        grad_out
        + second_scale * weighted
        - scaled_hidden
        * second_scale
        * second_scale
        * jnp.mean(weighted * hidden, axis=-1, keepdims=True)
    )
    grad_group = lax.all_gather(grad_hidden.astype(BF16), "tensor", axis=0, tiled=True)
    part_out, part_in, grad_group = lax.optimization_barrier((part_out, part_in, grad_group))
    grad_expert_out = lax.psum_scatter(
        part_out, "tensor", scatter_dimension=0, tiled=True
    ).astype(F32)
    grad_expert_in = lax.psum_scatter(part_in, "tensor", scatter_dimension=0, tiled=True).astype(
        F32
    )

    dx_part, gw_part, drv, grad_first = attend_back(
        xn1, grad_group, w_heads, rv, segc, segr, qkv, mixed, lse, xin, r1_all, head_dim
    )
    grad_first_in = lax.psum_scatter(dx_part, "tensor", scatter_dimension=0, tiled=True).astype(F32)
    first_scale = rms_scale(input_f)
    weighted_one = grad_first_in * first_f
    grad_inputs = (
        grad_hidden
        + first_scale * weighted_one
        - input_f
        * first_scale
        * first_scale
        * first_scale
        * jnp.mean(weighted_one * input_f, axis=-1, keepdims=True)
    )

    gw = lax.psum_scatter(
        jnp.transpose(gw_part, (1, 0, 2)), "dp", scatter_dimension=0, tiled=True
    ).astype(F32)
    grad_qkv_shard = gw[:, :, :triple]
    grad_out_shard = jnp.transpose(gw[:, :, triple:].reshape(rows_dp, heads_dev * head_dim))

    drv_gap = drv[:, 0, ::-1]
    table = jnp.sum(jnp.where(onehot_bucket[None], drv_gap[:, :, None], 0.0), axis=1)
    tensor_at = lax.axis_index("tensor")
    dp_at = lax.axis_index("dp")
    table_all = jnp.where(
        (jnp.arange(n_tensor) == tensor_at)[:, None, None], jnp.transpose(table)[None], 0.0
    )
    small = jnp.concatenate(
        [
            grad_first.reshape(-1),
            grad_second,
            grad_router.reshape(-1),
            table_all.reshape(-1),
        ]
    )
    small = lax.psum(small, ("dp", "tensor"))
    per_dev = model_width // (n_dp * n_tensor)
    own = (dp_at * n_tensor + tensor_at) * per_dev
    grad_first_shard = lax.dynamic_slice(small, (own,), (per_dev,))
    grad_second_shard = lax.dynamic_slice(small, (model_width + own,), (per_dev,))
    grad_router_shard = lax.dynamic_slice(
        small, (2 * model_width + own * experts,), (per_dev * experts,)
    ).reshape(per_dev, experts)
    table_size = bucket_count * heads_dev
    table_base = 2 * model_width + model_width * experts
    grad_table = lax.dynamic_slice(
        small, (table_base + tensor_at * table_size,), (table_size,)
    ).reshape(bucket_count, heads_dev)
    return (
        result,
        grad_inputs,
        grad_first_shard,
        grad_qkv_shard,
        grad_out_shard,
        grad_table,
        grad_second_shard,
        grad_router_shard,
        grad_expert_in,
        grad_expert_out,
    )


def solution(mesh):
    return jax.shard_map(
        body,
        mesh=mesh,
        in_specs=(
            P(("dp", "tensor"), None),
            P("dp"),
            P("dp", "tensor", None),
            P("tensor", "dp"),
            P(None, "tensor"),
            P("dp"),
            P("dp", None),
            P("dp", None, "tensor"),
            P("dp", "tensor", None),
            P("dp", None),
            P(),
            P(("dp", "tensor"), None),
            P(("dp", "tensor"), None),
        ),
        out_specs=(
            P(("dp", "tensor"), None),
            P(("dp", "tensor"), None),
            P(("dp", "tensor")),
            P("dp", "tensor", None),
            P("tensor", "dp"),
            P(None, "tensor"),
            P(("dp", "tensor")),
            P(("dp", "tensor"), None),
            P("dp", None, "tensor"),
            P("dp", "tensor", None),
        ),
        check_vma=False,
    )
```

```python
import functools

import jax
import jax.numpy as jnp
from jax import lax
from jax.experimental import pallas as pl
from jax.experimental.pallas import tpu as pltpu
from jax.sharding import PartitionSpec as P

EPSILON = 1e-06
MASKED = -1e30
TILE = 256
F32 = jnp.float32
BF16 = jnp.bfloat16


def rms_scale(values):
    return lax.rsqrt(jnp.mean(values * values, axis=-1, keepdims=True) + EPSILON)


def dot_nn(a, b):
    return lax.dot_general(a, b, (((1,), (0,)), ((), ())), preferred_element_type=F32)


def dot_nt(a, b):
    return lax.dot_general(a, b, (((1,), (1,)), ((), ())), preferred_element_type=F32)


def dot_tn(a, b):
    return lax.dot_general(a, b, (((0,), (0,)), ((), ())), preferred_element_type=F32)


def tile_mask(segc_ref, segr_ref, start, keys):
    rows = start + lax.broadcasted_iota(jnp.int32, (TILE, keys), 0)
    cols = lax.broadcasted_iota(jnp.int32, (TILE, keys), 1)
    same = segc_ref[start : start + TILE, :] == segr_ref[:, :keys]
    return (cols <= rows) & same


def toeplitz(rv_row, length):
    return pltpu.roll(
        jnp.broadcast_to(rv_row, (TILE, length)), length - TILE + 1, 1, stride=1, stride_axis=0
    )


def attend_kernel(
    head_dim, x_ref, w_ref, rv_ref, segc_ref, segr_ref, part_ref, qkv_ref, o_ref, lse_ref, acc_ref
):
    head = pl.program_id(0)
    length = x_ref.shape[0]
    w = w_ref[0]
    qkv = dot_nn(x_ref[...], w[:, : 3 * head_dim]).astype(BF16)
    qkv_ref[0] = qkv
    scaled = qkv[:, :head_dim] * jnp.asarray(head_dim ** (-0.5), BF16)
    keys = qkv[:, head_dim : 2 * head_dim]
    vals = qkv[:, 2 * head_dim :]
    bias = toeplitz(rv_ref[0], length)
    for start in range(0, length, TILE):
        stop = start + TILE
        s = dot_nt(scaled[start:stop], keys[:stop]) + bias[:, length - stop :]
        s = jnp.where(tile_mask(segc_ref, segr_ref, start, stop), s, MASKED)
        top = jnp.max(s, axis=-1, keepdims=True)
        e = jnp.exp(s - top)
        total = jnp.sum(e, axis=-1, keepdims=True)
        p = (e * (1.0 / total)).astype(BF16)
        o_ref[0, start:stop, :] = dot_nn(p, vals[:stop]).astype(BF16)
        lse_ref[0, start:stop, :] = top + jnp.log(total)
    out_t = w[:, 3 * head_dim :]
    part = dot_nt(o_ref[0], out_t)

    @pl.when(head == 0)
    def _():
        acc_ref[...] = part

    @pl.when(head > 0)
    def _():
        acc_ref[...] += part

    @pl.when(head == pl.num_programs(0) - 1)
    def _():
        part_ref[...] = acc_ref[...].astype(BF16)


def attend_back_kernel(
    head_dim,
    x_ref,
    g_ref,
    w_ref,
    rv_ref,
    segc_ref,
    segr_ref,
    qkv_ref,
    o_ref,
    lse_ref,
    xin_ref,
    r1_ref,
    dx_ref,
    gw_ref,
    drv_ref,
    gfirst_ref,
    acc_ref,
    diag_ref,
    dqkv_ref,
):
    head = pl.program_id(0)
    length = x_ref.shape[0]
    w = w_ref[0]
    qkv = qkv_ref[0]
    factor = head_dim ** (-0.5)
    grad_o = dot_nn(g_ref[...], w[:, 3 * head_dim :]).astype(BF16)
    scaled = qkv[:, :head_dim] * jnp.asarray(factor, BF16)
    keys = qkv[:, head_dim : 2 * head_dim]
    vals = qkv[:, 2 * head_dim :]
    bias = toeplitz(rv_ref[0], length)
    dkv = [None] * (length // TILE)
    diag_ref[...] = jnp.zeros_like(diag_ref)
    for start in range(0, length, TILE):
        stop = start + TILE
        s = dot_nt(scaled[start:stop], keys[:stop]) + bias[:, length - stop :]
        s = jnp.where(tile_mask(segc_ref, segr_ref, start, stop), s, MASKED)
        p = jnp.exp(s - lse_ref[0, start:stop, :])
        do = grad_o[start:stop]
        dp = dot_nt(do, vals[:stop])
        delta = jnp.sum(p * dp, axis=-1, keepdims=True)
        ds = (p * (dp - delta)).astype(BF16)
        diag_ref[:, length - stop :] += ds.astype(F32)
        dqkv_ref[start:stop, :head_dim] = dot_nn(ds, keys[:stop]) * factor
        dk = dot_tn(ds, scaled[start:stop])
        dv = dot_tn(p.astype(BF16), do)
        both = jnp.concatenate([dk, dv], axis=1)
        if start == 0:
            dqkv_ref[:stop, head_dim:] = both
        else:
            dqkv_ref[:start, head_dim:] += both[:start]
            dqkv_ref[start:stop, head_dim:] = both[start:]
    x = diag_ref[...]
    half = TILE // 2
    while half >= 8:
        x = x[:half] + pltpu.roll(x[half : 2 * half], length - half, 1)
        half //= 2
    total = x[0:1]
    for row in range(1, 8):
        total = total + pltpu.roll(x[row : row + 1], length - row, 1)
    drv_ref[0] = pltpu.roll(total, TILE - 1, 1)
    dqkv = dqkv_ref[...].astype(BF16)
    gw_ref[0, :, : 3 * head_dim] = dot_tn(x_ref[...], dqkv).astype(gw_ref.dtype)
    gw_ref[0, :, 3 * head_dim :] = dot_tn(g_ref[...], o_ref[0]).astype(gw_ref.dtype)
    part = dot_nt(dqkv, w[:, : 3 * head_dim])

    @pl.when(head == 0)
    def _():
        acc_ref[...] = part

    @pl.when(head > 0)
    def _():
        acc_ref[...] += part

    @pl.when(head == pl.num_programs(0) - 1)
    def _():
        full = acc_ref[...]
        dx_ref[...] = full.astype(BF16)
        gfirst_ref[...] = jnp.sum(
            full * (xin_ref[...].astype(F32) * r1_ref[...]), axis=0, keepdims=True
        )


def whole(shape):
    return pl.BlockSpec(shape, lambda h: (0,) * len(shape))


def by_head(shape):
    return pl.BlockSpec((1,) + shape, lambda h: (h,) + (0,) * len(shape))


def attend(x, w, rv, segc, segr, head_dim):
    heads = w.shape[0]
    length, width = x.shape
    return pl.pallas_call(
        functools.partial(attend_kernel, head_dim),
        grid=(heads,),
        in_specs=[
            whole(x.shape),
            by_head(w.shape[1:]),
            by_head((1, length)),
            whole(segc.shape),
            whole(segr.shape),
        ],
        out_specs=[
            whole(x.shape),
            by_head((length, 3 * head_dim)),
            by_head((length, head_dim)),
            by_head((length, 1)),
        ],
        out_shape=[
            jax.ShapeDtypeStruct(x.shape, BF16),
            jax.ShapeDtypeStruct((heads, length, 3 * head_dim), BF16),
            jax.ShapeDtypeStruct((heads, length, head_dim), BF16),
            jax.ShapeDtypeStruct((heads, length, 1), F32),
        ],
        scratch_shapes=[pltpu.VMEM(x.shape, F32)],
        compiler_params=pltpu.CompilerParams(vmem_limit_bytes=40 * 2**20),
        cost_estimate=pl.CostEstimate(
            flops=15_000_000_000, bytes_accessed=8_000_000, transcendentals=2_000_000
        ),
    )(x, w, rv, segc, segr)


def attend_back(x, g, w, rv, segc, segr, qkv, o, lse, xin, r1, head_dim):
    heads = w.shape[0]
    length, width = x.shape
    return pl.pallas_call(
        functools.partial(attend_back_kernel, head_dim),
        grid=(heads,),
        in_specs=[
            whole(x.shape),
            whole(g.shape),
            by_head(w.shape[1:]),
            by_head((1, length)),
            whole(segc.shape),
            whole(segr.shape),
            by_head(qkv.shape[1:]),
            by_head(o.shape[1:]),
            by_head(lse.shape[1:]),
            whole(xin.shape),
            whole(r1.shape),
        ],
        out_specs=[
            whole(x.shape),
            by_head(w.shape[1:]),
            by_head((1, length)),
            whole((1, width)),
        ],
        out_shape=[
            jax.ShapeDtypeStruct(x.shape, BF16),
            jax.ShapeDtypeStruct(w.shape, BF16),
            jax.ShapeDtypeStruct((heads, 1, length), F32),
            jax.ShapeDtypeStruct((1, width), F32),
        ],
        scratch_shapes=[
            pltpu.VMEM(x.shape, F32),
            pltpu.VMEM((TILE, length), F32),
            pltpu.VMEM((length, 3 * head_dim), F32),
        ],
        compiler_params=pltpu.CompilerParams(vmem_limit_bytes=48 * 2**20),
        cost_estimate=pl.CostEstimate(
            flops=30_000_000_000, bytes_accessed=16_000_000, transcendentals=2_000_000
        ),
    )(x, g, w, rv, segc, segr, qkv, o, lse, xin, r1)


def device_at(axis, offset, n_dp, n_tensor):
    dp_at, tensor_at = lax.axis_index("dp"), lax.axis_index("tensor")
    if axis == "dp":
        at = lax.rem(dp_at + offset, n_dp)
        return at, (at, tensor_at)
    if axis == "tensor":
        at = lax.rem(tensor_at + offset, n_tensor)
        return at, (dp_at, at)
    at = lax.rem(dp_at * n_tensor + tensor_at + offset, n_dp * n_tensor)
    return at, (lax.div(at, n_tensor), lax.rem(at, n_tensor))


def exchange_kernel(kinds, n_dp, n_tensor, *refs):
    count = len(kinds)
    srcs, dsts, sems = refs[:count], refs[count : 2 * count], refs[2 * count :]
    sizes = {"dp": n_dp, "tensor": n_tensor, "all": n_dp * n_tensor}
    axes = {axis for axis, _ in kinds}
    greeted = ["all"] if "all" in axes else sorted(axes)
    barrier = pltpu.get_barrier_semaphore()
    for axis in greeted:

        @pl.loop(1, sizes[axis])
        def _(offset, axis=axis):
            _, device = device_at(axis, offset, n_dp, n_tensor)
            pl.semaphore_signal(
                barrier, inc=1, device_id=device, device_id_type=pl.DeviceIdType.MESH
            )

    pl.semaphore_wait(barrier, sum(sizes[axis] - 1 for axis in greeted))

    def remote(item, offset, own):
        axis, swap = kinds[item]
        send_sem, recv_sem, _ = sems[3 * item : 3 * item + 3]
        at, device = device_at(axis, offset, n_dp, n_tensor)
        return pltpu.make_async_remote_copy(
            src_ref=srcs[item].at[at] if swap else srcs[item],
            dst_ref=dsts[item].at[own],
            send_sem=send_sem.at[offset],
            recv_sem=recv_sem.at[offset],
            device_id=device,
            device_id_type=pl.DeviceIdType.MESH,
        )

    local = []
    for item, (axis, swap) in enumerate(kinds):
        mine, _ = device_at(axis, 0, n_dp, n_tensor)

        @pl.loop(1, sizes[axis])
        def _(offset, item=item, mine=mine):
            remote(item, offset, mine).start()

        copy = pltpu.make_async_copy(
            srcs[item].at[mine] if swap else srcs[item],
            dsts[item].at[mine],
            sems[3 * item + 2],
        )
        copy.start()
        local.append(copy)
    for item, (axis, swap) in enumerate(kinds):
        local[item].wait()

        @pl.loop(1, sizes[axis])
        def _(offset, item=item, axis=axis):
            sender, _ = device_at(axis, sizes[axis] - offset, n_dp, n_tensor)
            copy = remote(item, offset, sender)
            copy.wait_recv()
            copy.wait_send()


def exchange(items, collective_id):
    n_dp, n_tensor = lax.axis_size("dp"), lax.axis_size("tensor")
    sizes = {"dp": n_dp, "tensor": n_tensor, "all": n_dp * n_tensor}
    kinds = tuple((axis, swap) for _, axis, swap in items)
    arrays = [array for array, _, _ in items]
    shapes = [
        jax.ShapeDtypeStruct(
            array.shape if swap else (sizes[axis],) + array.shape, array.dtype
        )
        for array, axis, swap in items
    ]
    scratch = []
    for axis, _ in kinds:
        scratch += [
            pltpu.SemaphoreType.DMA((sizes[axis],)),
            pltpu.SemaphoreType.DMA((sizes[axis],)),
            pltpu.SemaphoreType.DMA,
        ]
    return pl.pallas_call(
        functools.partial(exchange_kernel, kinds, n_dp, n_tensor),
        in_specs=[pl.BlockSpec(memory_space=pl.ANY)] * len(arrays),
        out_specs=[pl.BlockSpec(memory_space=pl.ANY)] * len(arrays),
        out_shape=shapes,
        scratch_shapes=scratch,
        compiler_params=pltpu.CompilerParams(
            collective_id=collective_id, has_side_effects=True
        ),
    )(*arrays)


def pad_rows(array, axis):
    extra = -array.shape[axis] % 16
    if extra == 0:
        return array
    widths = [(0, 0)] * array.ndim
    widths[axis] = (0, extra)
    return jnp.pad(array, widths)


def to_partner(array, flip):
    n_tensor = lax.axis_size("tensor")
    return lax.ppermute(array, "tensor", [(i, i ^ flip) for i in range(n_tensor)])


def gather_quarters(own):
    far = to_partner(own, 2)
    return [own, to_partner(own, 1), far, to_partner(far, 1)]


def sum_quarters(parts):
    near = to_partner(parts[1], 1)
    far = to_partner(parts[3], 1)
    send = (parts[2].astype(F32) + far.astype(F32)).astype(BF16)
    return parts[0].astype(F32) + near.astype(F32) + to_partner(send, 2).astype(F32)


def swap_dp(rows):
    return lax.all_to_all(rows, "dp", split_axis=0, concat_axis=0, tiled=True)


def body(
    inputs,
    first_gain,
    qkv_weight,
    out_weight,
    bias_table,
    second_gain,
    router_weight,
    expert_in,
    expert_output_weights,
    segments,
    buckets,
    choices,
    cotangent,
):
    tokens_dev, model_width = inputs.shape
    n_dp = lax.axis_size("dp")
    n_tensor = lax.axis_size("tensor")
    rows_dp, heads_dev, triple = qkv_weight.shape
    head_dim = triple // 3
    experts = router_weight.shape[1]
    seq_len = segments.shape[1]
    bucket_count = bias_table.shape[0]
    top_count = choices.shape[1]
    capacity = max(2, 2 * top_count * tokens_dev // experts)
    slots = experts * capacity

    packed = jnp.concatenate(
        [
            jnp.concatenate(
                [
                    qkv_weight,
                    jnp.transpose(out_weight).reshape(rows_dp, heads_dev, head_dim),
                ],
                axis=2,
            ).reshape(rows_dp, heads_dev * 4 * head_dim),
            first_gain[:, None],
            second_gain[:, None],
            router_weight,
        ],
        axis=1,
    )
    packed = pad_rows(jnp.pad(packed, ((0, 0), (0, -packed.shape[1] % 128))), 0)
    xin, shared = exchange([(inputs, "tensor", False), (packed, "dp", False)], 0)
    xin = xin.reshape(seq_len, model_width)
    shared = shared[:, :rows_dp].reshape(model_width, -1)
    wide = heads_dev * 4 * head_dim
    w_heads = jnp.transpose(
        shared[:, :wide].reshape(model_width, heads_dev, 4 * head_dim), (1, 0, 2)
    )
    first_f = shared[:, wide].astype(F32)
    second_f = shared[:, wide + 1].astype(F32)
    router_full = shared[:, wide + 2 : wide + 2 + experts]

    ein, eout, xin = lax.optimization_barrier((expert_in, expert_output_weights, xin))
    w_in = gather_quarters(ein[0])
    w_out = gather_quarters(eout[0])

    onehot_bucket = buckets[:, None] == jnp.arange(bucket_count, dtype=jnp.int32)[None, :]
    by_gap = jnp.sum(
        jnp.where(onehot_bucket[:, None, :], jnp.transpose(bias_table)[None].astype(F32), 0.0),
        axis=2,
    )
    rv = jnp.transpose(by_gap[::-1])[:, None, :]

    xin_f = xin.astype(F32)
    r1_all = rms_scale(xin_f)
    xn1 = (xin_f * r1_all * first_f).astype(BF16)
    segc = segments.reshape(seq_len, 1)
    segr = segments.reshape(1, seq_len)
    part, qkv, mixed, lse = attend(xn1, w_heads, rv, segc, segr, head_dim)
    (part,) = exchange([(part.reshape(n_tensor, tokens_dev, model_width), "tensor", True)], 1)
    attn = jnp.sum(part.astype(F32), axis=0)

    input_f = inputs.astype(F32)
    hidden = input_f + attn
    second_scale = rms_scale(hidden)
    normed_two = (hidden * second_scale * second_f).astype(BF16)
    logits = jnp.dot(normed_two, router_full, preferred_element_type=F32)
    probs = jax.nn.softmax(logits, axis=-1)

    pair_count = tokens_dev * top_count
    expert_range = jnp.arange(experts, dtype=jnp.int32)
    named = choices[:, :, None] == expert_range[None, None, :]
    named_flat = named.reshape(pair_count, experts)
    order = jnp.arange(pair_count, dtype=jnp.int32)
    earlier = (order[:, None] > order[None, :]).astype(BF16)
    before = jnp.dot(earlier, named_flat.astype(BF16), preferred_element_type=F32)
    slot = jnp.sum(jnp.where(named_flat, before, 0.0), axis=1).astype(jnp.int32)
    target = choices * capacity + slot.reshape(choices.shape)
    slot_range = jnp.arange(slots, dtype=jnp.int32)
    places = [(target[:, k : k + 1] == slot_range[None, :]).astype(BF16) for k in range(top_count)]

    picked = jnp.sum(jnp.where(named, probs[:, None, :], 0.0), axis=2)
    gate_sum = jnp.sum(picked, axis=1, keepdims=True)
    gates = picked / gate_sum
    grad_out = cotangent.astype(F32)

    send_rows = dot_tn(sum(places[1:], places[0]), normed_two).astype(BF16)
    grad_pairs = jnp.concatenate(
        [(gates[:, k : k + 1] * grad_out).astype(BF16) for k in range(top_count)], axis=0
    )
    send_grad = dot_tn(jnp.concatenate(places, axis=0), grad_pairs).astype(BF16)
    rows, grads = exchange(
        [
            (send_rows.reshape(n_dp, capacity, model_width), "dp", True),
            (send_grad.reshape(n_dp, capacity, model_width), "dp", True),
        ],
        2,
    )
    rows = rows.reshape(slots, model_width)
    grads = grads.reshape(slots, model_width)

    quarters = range(n_tensor)
    up = [dot_nn(rows, w_in[q]) for q in quarters]
    active = [jax.nn.gelu(up[q]).astype(BF16) for q in quarters]
    y = sum(dot_nn(active[q], w_out[q]) for q in quarters).astype(BF16)
    y_back = swap_dp(y.reshape(experts, capacity, model_width)).reshape(slots, model_width)
    grad_active = [dot_nt(grads, w_out[q]) for q in quarters]
    grad_up = [jax.vjp(jax.nn.gelu, up[q])[1](grad_active[q])[0].astype(BF16) for q in quarters]
    grad_rows = sum(dot_nt(grad_up[q], w_in[q]) for q in quarters).astype(BF16)
    grad_back = swap_dp(grad_rows.reshape(experts, capacity, model_width))
    grad_back = grad_back.reshape(slots, model_width)
    grad_expert_out = sum_quarters([dot_tn(active[q], grads).astype(BF16) for q in quarters])[None]
    grad_expert_in = sum_quarters([dot_tn(rows, grad_up[q]).astype(BF16) for q in quarters])[None]

    per_choice = [dot_nn(place, y_back) for place in places]
    result = hidden + sum(gates[:, k : k + 1] * per_choice[k] for k in range(top_count))
    grad_gate = jnp.concatenate(
        [jnp.sum(item * grad_out, axis=1, keepdims=True) for item in per_choice], axis=1
    )
    grad_picked = (grad_gate - jnp.sum(gates * grad_gate, axis=1, keepdims=True)) / gate_sum
    grad_probs = jnp.sum(jnp.where(named, grad_picked[:, :, None], 0.0), axis=1)
    grad_logits = (
        probs * (grad_probs - jnp.sum(probs * grad_probs, axis=1, keepdims=True))
    ).astype(BF16)
    grad_router = dot_tn(normed_two, grad_logits)
    grad_normed = dot_nt(grad_logits, router_full) + dot_nn(
        sum(places[1:], places[0]), grad_back
    )
    weighted = grad_normed * second_f
    scaled_hidden = hidden * second_scale
    grad_second = jnp.sum(grad_normed * scaled_hidden, axis=0)
    grad_hidden = (
        grad_out
        + second_scale * weighted
        - scaled_hidden
        * second_scale
        * second_scale
        * jnp.mean(weighted * hidden, axis=-1, keepdims=True)
    )
    (grad_group,) = exchange([(grad_hidden.astype(BF16), "tensor", False)], 3)
    grad_group = grad_group.reshape(seq_len, model_width)

    dx_part, gw_part, drv, grad_first = attend_back(
        xn1, grad_group, w_heads, rv, segc, segr, qkv, mixed, lse, xin, r1_all, head_dim
    )
    drv_gap = drv[:, 0, ::-1]
    table = jnp.sum(jnp.where(onehot_bucket[None], drv_gap[:, :, None], 0.0), axis=1)
    n_all = n_dp * n_tensor
    per_dev = model_width // n_all
    by_width = jnp.concatenate(
        [grad_first.reshape(-1, 1), grad_second[:, None], grad_router], axis=1
    ).reshape(n_all, 1, -1)
    small_size = by_width.shape[2]
    by_width = jnp.pad(by_width, ((0, 0), (0, 7), (0, -small_size % 128)))
    table_pad = jnp.pad(table, ((0, -heads_dev % 8), (0, -bucket_count % 128)))
    gw_rows = jnp.transpose(gw_part, (1, 0, 2)).reshape(n_dp, rows_dp, wide)
    dx_all, gw_all, table_all, small_all = exchange(
        [
            (dx_part.reshape(n_tensor, tokens_dev, model_width), "tensor", True),
            (pad_rows(gw_rows, 1), "dp", True),
            (table_pad, "dp", False),
            (by_width, "all", True),
        ],
        4,
    )
    grad_first_in = jnp.sum(dx_all.astype(F32), axis=0)
    gw = jnp.sum(gw_all[:, :rows_dp].astype(F32), axis=0)
    gw = gw.reshape(rows_dp, heads_dev, 4 * head_dim)
    grad_table = jnp.transpose(jnp.sum(table_all, axis=0)[:heads_dev, :bucket_count])
    small = jnp.sum(small_all[:, 0, :small_size], axis=0).reshape(per_dev, 2 + experts)
    grad_first_shard, grad_second_shard = small[:, 0], small[:, 1]
    grad_router_shard = small[:, 2:]
    first_scale = rms_scale(input_f)
    weighted_one = grad_first_in * first_f
    grad_inputs = (
        grad_hidden
        + first_scale * weighted_one
        - input_f
        * first_scale
        * first_scale
        * first_scale
        * jnp.mean(weighted_one * input_f, axis=-1, keepdims=True)
    )

    grad_qkv_shard = gw[:, :, :triple]
    grad_out_shard = jnp.transpose(gw[:, :, triple:].reshape(rows_dp, heads_dev * head_dim))

    return (
        result,
        grad_inputs,
        grad_first_shard,
        grad_qkv_shard,
        grad_out_shard,
        grad_table,
        grad_second_shard,
        grad_router_shard,
        grad_expert_in,
        grad_expert_out,
    )


def solution(mesh):
    return jax.shard_map(
        body,
        mesh=mesh,
        in_specs=(
            P(("dp", "tensor"), None),
            P("dp"),
            P("dp", "tensor", None),
            P("tensor", "dp"),
            P(None, "tensor"),
            P("dp"),
            P("dp", None),
            P("dp", None, "tensor"),
            P("dp", "tensor", None),
            P("dp", None),
            P(),
            P(("dp", "tensor"), None),
            P(("dp", "tensor"), None),
        ),
        out_specs=(
            P(("dp", "tensor"), None),
            P(("dp", "tensor"), None),
            P(("dp", "tensor")),
            P("dp", "tensor", None),
            P("tensor", "dp"),
            P(None, "tensor"),
            P(("dp", "tensor")),
            P(("dp", "tensor"), None),
            P("dp", None, "tensor"),
            P("dp", "tensor", None),
        ),
        check_vma=False,
    )
```

```python
import functools

import jax
import jax.numpy as jnp
from jax import lax
from jax.experimental import pallas as pl
from jax.experimental.pallas import tpu as pltpu
from jax.sharding import PartitionSpec as P

EPSILON = 1e-06
MASKED = -1e30
TILE = 256
F32 = jnp.float32
BF16 = jnp.bfloat16


def rms_scale(values):
    return lax.rsqrt(jnp.mean(values * values, axis=-1, keepdims=True) + EPSILON)


def dot_nn(a, b):
    return lax.dot_general(a, b, (((1,), (0,)), ((), ())), preferred_element_type=F32)


def dot_nt(a, b):
    return lax.dot_general(a, b, (((1,), (1,)), ((), ())), preferred_element_type=F32)


def dot_tn(a, b):
    return lax.dot_general(a, b, (((0,), (0,)), ((), ())), preferred_element_type=F32)


def tile_mask(segc_ref, segr_ref, start, keys):
    rows = start + lax.broadcasted_iota(jnp.int32, (TILE, keys), 0)
    cols = lax.broadcasted_iota(jnp.int32, (TILE, keys), 1)
    same = segc_ref[start : start + TILE, :] == segr_ref[:, :keys]
    return (cols <= rows) & same


def toeplitz(rv_row, length):
    return pltpu.roll(
        jnp.broadcast_to(rv_row, (TILE, length)), length - TILE + 1, 1, stride=1, stride_axis=0
    )


def attend_kernel(
    head_dim, x_ref, w_ref, rv_ref, segc_ref, segr_ref, part_ref, qkv_ref, o_ref, lse_ref, acc_ref
):
    head = pl.program_id(0)
    length = x_ref.shape[0]
    w = w_ref[0]
    qkv = dot_nn(x_ref[...], w[:, : 3 * head_dim]).astype(BF16)
    qkv_ref[0] = qkv
    scaled = qkv[:, :head_dim] * jnp.asarray(head_dim ** (-0.5), BF16)
    keys = qkv[:, head_dim : 2 * head_dim]
    vals = qkv[:, 2 * head_dim :]
    bias = toeplitz(rv_ref[0], length)
    for start in range(0, length, TILE):
        stop = start + TILE
        s = dot_nt(scaled[start:stop], keys[:stop]) + bias[:, length - stop :]
        s = jnp.where(tile_mask(segc_ref, segr_ref, start, stop), s, MASKED)
        top = jnp.max(s, axis=-1, keepdims=True)
        e = jnp.exp(s - top)
        total = jnp.sum(e, axis=-1, keepdims=True)
        p = (e * (1.0 / total)).astype(BF16)
        o_ref[0, start:stop, :] = dot_nn(p, vals[:stop]).astype(BF16)
        lse_ref[0, start:stop, :] = top + jnp.log(total)
    out_t = w[:, 3 * head_dim :]
    part = dot_nt(o_ref[0], out_t)

    @pl.when(head == 0)
    def _():
        acc_ref[...] = part

    @pl.when(head > 0)
    def _():
        acc_ref[...] += part

    @pl.when(head == pl.num_programs(0) - 1)
    def _():
        part_ref[...] = acc_ref[...].astype(BF16)


def attend_back_kernel(
    head_dim,
    x_ref,
    g_ref,
    w_ref,
    rv_ref,
    segc_ref,
    segr_ref,
    qkv_ref,
    o_ref,
    lse_ref,
    xin_ref,
    r1_ref,
    dx_ref,
    gw_ref,
    drv_ref,
    gfirst_ref,
    acc_ref,
    diag_ref,
    dqkv_ref,
):
    head = pl.program_id(0)
    length = x_ref.shape[0]
    w = w_ref[0]
    qkv = qkv_ref[0]
    factor = head_dim ** (-0.5)
    grad_o = dot_nn(g_ref[...], w[:, 3 * head_dim :]).astype(BF16)
    scaled = qkv[:, :head_dim] * jnp.asarray(factor, BF16)
    keys = qkv[:, head_dim : 2 * head_dim]
    vals = qkv[:, 2 * head_dim :]
    bias = toeplitz(rv_ref[0], length)
    dkv = [None] * (length // TILE)
    diag_ref[...] = jnp.zeros_like(diag_ref)
    for start in range(0, length, TILE):
        stop = start + TILE
        s = dot_nt(scaled[start:stop], keys[:stop]) + bias[:, length - stop :]
        s = jnp.where(tile_mask(segc_ref, segr_ref, start, stop), s, MASKED)
        p = jnp.exp(s - lse_ref[0, start:stop, :])
        do = grad_o[start:stop]
        dp = dot_nt(do, vals[:stop])
        delta = jnp.sum(p * dp, axis=-1, keepdims=True)
        ds = (p * (dp - delta)).astype(BF16)
        diag_ref[:, length - stop :] += ds.astype(F32)
        dqkv_ref[start:stop, :head_dim] = dot_nn(ds, keys[:stop]) * factor
        dk = dot_tn(ds, scaled[start:stop])
        dv = dot_tn(p.astype(BF16), do)
        both = jnp.concatenate([dk, dv], axis=1)
        if start == 0:
            dqkv_ref[:stop, head_dim:] = both
        else:
            dqkv_ref[:start, head_dim:] += both[:start]
            dqkv_ref[start:stop, head_dim:] = both[start:]
    x = diag_ref[...]
    half = TILE // 2
    while half >= 8:
        x = x[:half] + pltpu.roll(x[half : 2 * half], length - half, 1)
        half //= 2
    total = x[0:1]
    for row in range(1, 8):
        total = total + pltpu.roll(x[row : row + 1], length - row, 1)
    drv_ref[0] = pltpu.roll(total, TILE - 1, 1)
    dqkv = dqkv_ref[...].astype(BF16)
    gw_ref[0, :, : 3 * head_dim] = dot_tn(x_ref[...], dqkv).astype(gw_ref.dtype)
    gw_ref[0, :, 3 * head_dim :] = dot_tn(g_ref[...], o_ref[0]).astype(gw_ref.dtype)
    part = dot_nt(dqkv, w[:, : 3 * head_dim])

    @pl.when(head == 0)
    def _():
        acc_ref[...] = part

    @pl.when(head > 0)
    def _():
        acc_ref[...] += part

    @pl.when(head == pl.num_programs(0) - 1)
    def _():
        full = acc_ref[...]
        dx_ref[...] = full.astype(BF16)
        gfirst_ref[...] = jnp.sum(
            full * (xin_ref[...].astype(F32) * r1_ref[...]), axis=0, keepdims=True
        )


def expert_kernel(rows_ref, w_in_ref, w_out_ref, y_ref, active_ref, slope_ref, acc_ref):
    quarter = pl.program_id(0)
    root = (2.0 / 3.141592653589793) ** 0.5
    for start in range(0, rows_ref.shape[0], TILE):
        at = slice(start, start + TILE)
        u = dot_nn(rows_ref[at], w_in_ref[0])
        square = u * u
        t = jnp.tanh(u * (root + (root * 0.044715) * square))
        side = 0.5 + 0.5 * t
        active = (u * side).astype(BF16)
        active_ref[0, at] = active
        slope = side + 0.5 * u * (1.0 - t * t) * (root + (3.0 * 0.044715 * root) * square)
        slope_ref[0, at] = slope.astype(BF16)
        part = dot_nn(active, w_out_ref[0])

        @pl.when(quarter == 0)
        def _(at=at, part=part):
            acc_ref[at] = part

        @pl.when(quarter > 0)
        def _(at=at, part=part):
            acc_ref[at] += part

    @pl.when(quarter == pl.num_programs(0) - 1)
    def _():
        y_ref[...] = acc_ref[...].astype(BF16)


def expert_back_kernel(grads_ref, w_in_ref, w_out_ref, slope_ref, dx_ref, du_ref, acc_ref):
    quarter = pl.program_id(0)
    for start in range(0, grads_ref.shape[0], TILE):
        at = slice(start, start + TILE)
        da = dot_nt(grads_ref[at], w_out_ref[0])
        du = (da * slope_ref[0, at].astype(F32)).astype(BF16)
        du_ref[0, at] = du
        part = dot_nt(du, w_in_ref[0])

        @pl.when(quarter == 0)
        def _(at=at, part=part):
            acc_ref[at] = part

        @pl.when(quarter > 0)
        def _(at=at, part=part):
            acc_ref[at] += part

    @pl.when(quarter == pl.num_programs(0) - 1)
    def _():
        dx_ref[...] = acc_ref[...].astype(BF16)


def expert(rows, w_in, w_out):
    quarters, width, hidden = w_in.shape
    kept = jax.ShapeDtypeStruct((quarters, rows.shape[0], hidden), BF16)
    return pl.pallas_call(
        expert_kernel,
        grid=(quarters,),
        in_specs=[whole(rows.shape), by_head((width, hidden)), by_head((hidden, width))],
        out_specs=[whole(rows.shape), by_head(kept.shape[1:]), by_head(kept.shape[1:])],
        out_shape=[jax.ShapeDtypeStruct(rows.shape, BF16), kept, kept],
        scratch_shapes=[pltpu.VMEM(rows.shape, F32)],
        compiler_params=pltpu.CompilerParams(vmem_limit_bytes=40 * 2**20),
        cost_estimate=pl.CostEstimate(
            flops=20_000_000_000, bytes_accessed=25_000_000, transcendentals=3_000_000
        ),
    )(rows, w_in, w_out)


def expert_back(grads, w_in, w_out, slope):
    quarters, width, hidden = w_in.shape
    kept = jax.ShapeDtypeStruct(slope.shape, BF16)
    return pl.pallas_call(
        expert_back_kernel,
        grid=(quarters,),
        in_specs=[
            whole(grads.shape),
            by_head((width, hidden)),
            by_head((hidden, width)),
            by_head(slope.shape[1:]),
        ],
        out_specs=[whole(grads.shape), by_head(kept.shape[1:])],
        out_shape=[jax.ShapeDtypeStruct(grads.shape, BF16), kept],
        scratch_shapes=[pltpu.VMEM(grads.shape, F32)],
        compiler_params=pltpu.CompilerParams(vmem_limit_bytes=40 * 2**20),
        cost_estimate=pl.CostEstimate(
            flops=20_000_000_000, bytes_accessed=25_000_000, transcendentals=0
        ),
    )(grads, w_in, w_out, slope)


def whole(shape):
    return pl.BlockSpec(shape, lambda h: (0,) * len(shape))


def by_head(shape):
    return pl.BlockSpec((1,) + shape, lambda h: (h,) + (0,) * len(shape))


def attend(x, w, rv, segc, segr, head_dim):
    heads = w.shape[0]
    length, width = x.shape
    return pl.pallas_call(
        functools.partial(attend_kernel, head_dim),
        grid=(heads,),
        in_specs=[
            whole(x.shape),
            by_head(w.shape[1:]),
            by_head((1, length)),
            whole(segc.shape),
            whole(segr.shape),
        ],
        out_specs=[
            whole(x.shape),
            by_head((length, 3 * head_dim)),
            by_head((length, head_dim)),
            by_head((length, 1)),
        ],
        out_shape=[
            jax.ShapeDtypeStruct(x.shape, BF16),
            jax.ShapeDtypeStruct((heads, length, 3 * head_dim), BF16),
            jax.ShapeDtypeStruct((heads, length, head_dim), BF16),
            jax.ShapeDtypeStruct((heads, length, 1), F32),
        ],
        scratch_shapes=[pltpu.VMEM(x.shape, F32)],
        compiler_params=pltpu.CompilerParams(vmem_limit_bytes=40 * 2**20),
        cost_estimate=pl.CostEstimate(
            flops=15_000_000_000, bytes_accessed=8_000_000, transcendentals=2_000_000
        ),
    )(x, w, rv, segc, segr)


def attend_back(x, g, w, rv, segc, segr, qkv, o, lse, xin, r1, head_dim):
    heads = w.shape[0]
    length, width = x.shape
    return pl.pallas_call(
        functools.partial(attend_back_kernel, head_dim),
        grid=(heads,),
        in_specs=[
            whole(x.shape),
            whole(g.shape),
            by_head(w.shape[1:]),
            by_head((1, length)),
            whole(segc.shape),
            whole(segr.shape),
            by_head(qkv.shape[1:]),
            by_head(o.shape[1:]),
            by_head(lse.shape[1:]),
            whole(xin.shape),
            whole(r1.shape),
        ],
        out_specs=[
            whole(x.shape),
            by_head(w.shape[1:]),
            by_head((1, length)),
            whole((1, width)),
        ],
        out_shape=[
            jax.ShapeDtypeStruct(x.shape, BF16),
            jax.ShapeDtypeStruct(w.shape, BF16),
            jax.ShapeDtypeStruct((heads, 1, length), F32),
            jax.ShapeDtypeStruct((1, width), F32),
        ],
        scratch_shapes=[
            pltpu.VMEM(x.shape, F32),
            pltpu.VMEM((TILE, length), F32),
            pltpu.VMEM((length, 3 * head_dim), F32),
        ],
        compiler_params=pltpu.CompilerParams(vmem_limit_bytes=48 * 2**20),
        cost_estimate=pl.CostEstimate(
            flops=30_000_000_000, bytes_accessed=16_000_000, transcendentals=2_000_000
        ),
    )(x, g, w, rv, segc, segr, qkv, o, lse, xin, r1)


def device_at(axis, offset, n_dp, n_tensor):
    dp_at, tensor_at = lax.axis_index("dp"), lax.axis_index("tensor")
    if axis == "dp":
        at = lax.rem(dp_at + offset, n_dp)
        return at, (at, tensor_at)
    if axis == "tensor":
        at = lax.rem(tensor_at + offset, n_tensor)
        return at, (dp_at, at)
    at = lax.rem(dp_at * n_tensor + tensor_at + offset, n_dp * n_tensor)
    return at, (lax.div(at, n_tensor), lax.rem(at, n_tensor))


def exchange_kernel(kinds, n_dp, n_tensor, *refs):
    count = len(kinds)
    srcs, dsts, sems = refs[:count], refs[count : 2 * count], refs[2 * count :]
    sizes = {"dp": n_dp, "tensor": n_tensor, "all": n_dp * n_tensor}
    axes = {axis for axis, _ in kinds}
    greeted = ["all"] if "all" in axes else sorted(axes)
    barrier = pltpu.get_barrier_semaphore()
    for axis in greeted:

        @pl.loop(1, sizes[axis])
        def _(offset, axis=axis):
            _, device = device_at(axis, offset, n_dp, n_tensor)
            pl.semaphore_signal(
                barrier, inc=1, device_id=device, device_id_type=pl.DeviceIdType.MESH
            )

    pl.semaphore_wait(barrier, sum(sizes[axis] - 1 for axis in greeted))

    def remote(item, offset, own):
        axis, swap = kinds[item]
        send_sem, recv_sem, _ = sems[3 * item : 3 * item + 3]
        at, device = device_at(axis, offset, n_dp, n_tensor)
        return pltpu.make_async_remote_copy(
            src_ref=srcs[item].at[at] if swap else srcs[item],
            dst_ref=dsts[item].at[own],
            send_sem=send_sem.at[offset],
            recv_sem=recv_sem.at[offset],
            device_id=device,
            device_id_type=pl.DeviceIdType.MESH,
        )

    local = []
    for item, (axis, swap) in enumerate(kinds):
        mine, _ = device_at(axis, 0, n_dp, n_tensor)

        @pl.loop(1, sizes[axis])
        def _(offset, item=item, mine=mine):
            remote(item, offset, mine).start()

        copy = pltpu.make_async_copy(
            srcs[item].at[mine] if swap else srcs[item],
            dsts[item].at[mine],
            sems[3 * item + 2],
        )
        copy.start()
        local.append(copy)
    for item, (axis, swap) in enumerate(kinds):
        local[item].wait()

        @pl.loop(1, sizes[axis])
        def _(offset, item=item, axis=axis):
            sender, _ = device_at(axis, sizes[axis] - offset, n_dp, n_tensor)
            copy = remote(item, offset, sender)
            copy.wait_recv()
            copy.wait_send()


def exchange(items, collective_id):
    n_dp, n_tensor = lax.axis_size("dp"), lax.axis_size("tensor")
    sizes = {"dp": n_dp, "tensor": n_tensor, "all": n_dp * n_tensor}
    kinds = tuple((axis, swap) for _, axis, swap in items)
    arrays = [array for array, _, _ in items]
    shapes = [
        jax.ShapeDtypeStruct(
            array.shape if swap else (sizes[axis],) + array.shape, array.dtype
        )
        for array, axis, swap in items
    ]
    scratch = []
    for axis, _ in kinds:
        scratch += [
            pltpu.SemaphoreType.DMA((sizes[axis],)),
            pltpu.SemaphoreType.DMA((sizes[axis],)),
            pltpu.SemaphoreType.DMA,
        ]
    return pl.pallas_call(
        functools.partial(exchange_kernel, kinds, n_dp, n_tensor),
        in_specs=[pl.BlockSpec(memory_space=pl.ANY)] * len(arrays),
        out_specs=[pl.BlockSpec(memory_space=pl.ANY)] * len(arrays),
        out_shape=shapes,
        scratch_shapes=scratch,
        compiler_params=pltpu.CompilerParams(
            collective_id=collective_id, has_side_effects=True
        ),
    )(*arrays)


def pad_rows(array, axis):
    extra = -array.shape[axis] % 16
    if extra == 0:
        return array
    widths = [(0, 0)] * array.ndim
    widths[axis] = (0, extra)
    return jnp.pad(array, widths)


def to_partner(array, flip):
    n_tensor = lax.axis_size("tensor")
    return lax.ppermute(array, "tensor", [(i, i ^ flip) for i in range(n_tensor)])


def gather_quarters(own):
    far = to_partner(own, 2)
    return [own, to_partner(own, 1), far, to_partner(far, 1)]


def sum_near(parts):
    near = to_partner(parts[1], 1).astype(F32)
    far = to_partner(parts[3], 1).astype(F32)
    return parts[0].astype(F32) + near, (parts[2].astype(F32) + far).astype(BF16)


def swap_dp(rows):
    return lax.all_to_all(rows, "dp", split_axis=0, concat_axis=0, tiled=True)


def body(
    inputs,
    first_gain,
    qkv_weight,
    out_weight,
    bias_table,
    second_gain,
    router_weight,
    expert_in,
    expert_output_weights,
    segments,
    buckets,
    choices,
    cotangent,
):
    tokens_dev, model_width = inputs.shape
    n_dp = lax.axis_size("dp")
    n_tensor = lax.axis_size("tensor")
    rows_dp, heads_dev, triple = qkv_weight.shape
    head_dim = triple // 3
    experts = router_weight.shape[1]
    seq_len = segments.shape[1]
    bucket_count = bias_table.shape[0]
    top_count = choices.shape[1]
    capacity = max(2, 2 * top_count * tokens_dev // experts)
    slots = experts * capacity

    packed = jnp.concatenate(
        [
            jnp.concatenate(
                [
                    qkv_weight,
                    jnp.transpose(out_weight).reshape(rows_dp, heads_dev, head_dim),
                ],
                axis=2,
            ).reshape(rows_dp, heads_dev * 4 * head_dim),
            first_gain[:, None],
            second_gain[:, None],
            router_weight,
        ],
        axis=1,
    )
    packed = pad_rows(jnp.pad(packed, ((0, 0), (0, -packed.shape[1] % 128))), 0)
    xin, shared = exchange([(inputs, "tensor", False), (packed, "dp", False)], 0)
    xin = xin.reshape(seq_len, model_width)
    shared = shared[:, :rows_dp].reshape(model_width, -1)
    wide = heads_dev * 4 * head_dim
    w_heads = jnp.transpose(
        shared[:, :wide].reshape(model_width, heads_dev, 4 * head_dim), (1, 0, 2)
    )
    first_f = shared[:, wide].astype(F32)
    second_f = shared[:, wide + 1].astype(F32)
    router_full = shared[:, wide + 2 : wide + 2 + experts]

    onehot_bucket = buckets[:, None] == jnp.arange(bucket_count, dtype=jnp.int32)[None, :]
    by_gap = jnp.sum(
        jnp.where(onehot_bucket[:, None, :], jnp.transpose(bias_table)[None].astype(F32), 0.0),
        axis=2,
    )
    rv = jnp.transpose(by_gap[::-1])[:, None, :]

    xin_f = xin.astype(F32)
    r1_all = rms_scale(xin_f)
    xn1 = (xin_f * r1_all * first_f).astype(BF16)
    segc = segments.reshape(seq_len, 1)
    segr = segments.reshape(1, seq_len)
    part, qkv, mixed, lse = attend(xn1, w_heads, rv, segc, segr, head_dim)
    (part,) = exchange([(part.reshape(n_tensor, tokens_dev, model_width), "tensor", True)], 1)
    ein, eout, part = lax.optimization_barrier((expert_in, expert_output_weights, part))
    w_in = gather_quarters(ein[0])
    w_out = gather_quarters(eout[0])
    attn = jnp.sum(part.astype(F32), axis=0)

    input_f = inputs.astype(F32)
    hidden = input_f + attn
    second_scale = rms_scale(hidden)
    normed_two = (hidden * second_scale * second_f).astype(BF16)
    logits = jnp.dot(normed_two, router_full, preferred_element_type=F32)
    probs = jax.nn.softmax(logits, axis=-1)

    pair_count = tokens_dev * top_count
    expert_range = jnp.arange(experts, dtype=jnp.int32)
    named = choices[:, :, None] == expert_range[None, None, :]
    named_flat = named.reshape(pair_count, experts)
    order = jnp.arange(pair_count, dtype=jnp.int32)
    earlier = (order[:, None] > order[None, :]).astype(BF16)
    before = jnp.dot(earlier, named_flat.astype(BF16), preferred_element_type=F32)
    slot = jnp.sum(jnp.where(named_flat, before, 0.0), axis=1).astype(jnp.int32)
    target = choices * capacity + slot.reshape(choices.shape)
    slot_range = jnp.arange(slots, dtype=jnp.int32)
    places = [(target[:, k : k + 1] == slot_range[None, :]).astype(BF16) for k in range(top_count)]

    picked = jnp.sum(jnp.where(named, probs[:, None, :], 0.0), axis=2)
    gate_sum = jnp.sum(picked, axis=1, keepdims=True)
    gates = picked / gate_sum
    grad_out = cotangent.astype(F32)

    send_rows = dot_tn(sum(places[1:], places[0]), normed_two).astype(BF16)
    grad_pairs = jnp.concatenate(
        [(gates[:, k : k + 1] * grad_out).astype(BF16) for k in range(top_count)], axis=0
    )
    send_grad = dot_tn(jnp.concatenate(places, axis=0), grad_pairs).astype(BF16)
    send_rows = send_rows.reshape(n_dp, capacity, model_width)
    (rows,) = exchange([(send_rows, "dp", True)], 2)
    rows, send_grad = lax.optimization_barrier((rows, send_grad))
    rows = rows.reshape(slots, model_width)
    grads = swap_dp(send_grad.reshape(experts, capacity, model_width))
    grads = grads.reshape(slots, model_width)

    quarters = range(n_tensor)
    w_in, w_out = jnp.stack(w_in), jnp.stack(w_out)
    y, active, slope = expert(rows, w_in, w_out)
    y, grads = lax.optimization_barrier((y, grads))
    y_back = swap_dp(y.reshape(experts, capacity, model_width)).reshape(slots, model_width)
    grad_rows, grad_up = expert_back(grads, w_in, w_out, slope)
    grad_back = swap_dp(grad_rows.reshape(experts, capacity, model_width))
    grad_back = grad_back.reshape(slots, model_width)
    out_keep, out_send = sum_near([dot_tn(active[q], grads).astype(BF16) for q in quarters])
    in_keep, in_send = sum_near([dot_tn(rows, grad_up[q]).astype(BF16) for q in quarters])

    per_choice = [dot_nn(place, y_back) for place in places]
    result = hidden + sum(gates[:, k : k + 1] * per_choice[k] for k in range(top_count))
    grad_gate = jnp.concatenate(
        [jnp.sum(item * grad_out, axis=1, keepdims=True) for item in per_choice], axis=1
    )
    grad_picked = (grad_gate - jnp.sum(gates * grad_gate, axis=1, keepdims=True)) / gate_sum
    grad_probs = jnp.sum(jnp.where(named, grad_picked[:, :, None], 0.0), axis=1)
    grad_logits = (
        probs * (grad_probs - jnp.sum(probs * grad_probs, axis=1, keepdims=True))
    ).astype(BF16)
    grad_router = dot_tn(normed_two, grad_logits)
    grad_normed = dot_nt(grad_logits, router_full) + dot_nn(
        sum(places[1:], places[0]), grad_back
    )
    weighted = grad_normed * second_f
    scaled_hidden = hidden * second_scale
    grad_second = jnp.sum(grad_normed * scaled_hidden, axis=0)
    grad_hidden = (
        grad_out
        + second_scale * weighted
        - scaled_hidden
        * second_scale
        * second_scale
        * jnp.mean(weighted * hidden, axis=-1, keepdims=True)
    )
    out_send, in_send, grad_low = lax.optimization_barrier(
        (out_send, in_send, grad_hidden.astype(BF16))
    )
    (grad_group,) = exchange([(grad_low, "tensor", False)], 3)
    out_send, in_send, grad_group = lax.optimization_barrier((out_send, in_send, grad_group))
    out_far, in_far = to_partner(out_send, 2), to_partner(in_send, 2)
    grad_group = grad_group.reshape(seq_len, model_width)

    dx_part, gw_part, drv, grad_first = attend_back(
        xn1, grad_group, w_heads, rv, segc, segr, qkv, mixed, lse, xin, r1_all, head_dim
    )
    out_far, in_far, dx_part = lax.optimization_barrier((out_far, in_far, dx_part))

    drv_gap = drv[:, 0, ::-1]
    table = jnp.sum(jnp.where(onehot_bucket[None], drv_gap[:, :, None], 0.0), axis=1)
    n_all = n_dp * n_tensor
    per_dev = model_width // n_all
    by_width = jnp.concatenate(
        [grad_first.reshape(-1, 1), grad_second[:, None], grad_router], axis=1
    ).reshape(n_all, 1, -1)
    small_size = by_width.shape[2]
    by_width = jnp.pad(by_width, ((0, 0), (0, 7), (0, -small_size % 128)))
    table_pad = jnp.pad(table, ((0, -heads_dev % 8), (0, -bucket_count % 128)))
    gw_rows = jnp.transpose(gw_part, (1, 0, 2)).reshape(n_dp, rows_dp, wide)
    dx_all, gw_all, table_all, small_all = exchange(
        [
            (dx_part.reshape(n_tensor, tokens_dev, model_width), "tensor", True),
            (pad_rows(gw_rows, 1), "dp", True),
            (table_pad, "dp", False),
            (by_width, "all", True),
        ],
        4,
    )
    grad_first_in = jnp.sum(dx_all.astype(F32), axis=0)
    gw = jnp.sum(gw_all[:, :rows_dp].astype(F32), axis=0)
    gw = gw.reshape(rows_dp, heads_dev, 4 * head_dim)
    grad_table = jnp.transpose(jnp.sum(table_all, axis=0)[:heads_dev, :bucket_count])
    small = jnp.sum(small_all[:, 0, :small_size], axis=0).reshape(per_dev, 2 + experts)
    grad_first_shard, grad_second_shard = small[:, 0], small[:, 1]
    grad_router_shard = small[:, 2:]
    grad_expert_out = (out_keep + out_far.astype(F32))[None]
    grad_expert_in = (in_keep + in_far.astype(F32))[None]
    first_scale = rms_scale(input_f)
    weighted_one = grad_first_in * first_f
    grad_inputs = (
        grad_hidden
        + first_scale * weighted_one
        - input_f
        * first_scale
        * first_scale
        * first_scale
        * jnp.mean(weighted_one * input_f, axis=-1, keepdims=True)
    )

    grad_qkv_shard = gw[:, :, :triple]
    grad_out_shard = jnp.transpose(gw[:, :, triple:].reshape(rows_dp, heads_dev * head_dim))

    return (
        result,
        grad_inputs,
        grad_first_shard,
        grad_qkv_shard,
        grad_out_shard,
        grad_table,
        grad_second_shard,
        grad_router_shard,
        grad_expert_in,
        grad_expert_out,
    )


def solution(mesh):
    return jax.shard_map(
        body,
        mesh=mesh,
        in_specs=(
            P(("dp", "tensor"), None),
            P("dp"),
            P("dp", "tensor", None),
            P("tensor", "dp"),
            P(None, "tensor"),
            P("dp"),
            P("dp", None),
            P("dp", None, "tensor"),
            P("dp", "tensor", None),
            P("dp", None),
            P(),
            P(("dp", "tensor"), None),
            P(("dp", "tensor"), None),
        ),
        out_specs=(
            P(("dp", "tensor"), None),
            P(("dp", "tensor"), None),
            P(("dp", "tensor")),
            P("dp", "tensor", None),
            P("tensor", "dp"),
            P(None, "tensor"),
            P(("dp", "tensor")),
            P(("dp", "tensor"), None),
            P("dp", None, "tensor"),
            P("dp", "tensor", None),
        ),
        check_vma=False,
    )
```
